1024 devices in a mesh: ep: 32 (over z, y_lo), rep: 32 (over y_hi, x, core).
Axes of the slice: x: 8, y: 8 (y_hi: 2, y_lo: 4; y = y_hi * 4 + y_lo), z: 8, core: 2. Of those that a mesh axis runs over, the one named last changes fastest.
Arguments:
- tokens: bfloat16 [1536, 4096], P('ep'), may hold values from -6 to 6
- cotangent: bfloat16 [1536, 4096], P('ep'), may hold values from -6 to 6
- routes: int32 [1536, 8], P('ep'), may hold values from 0 to 127, all different within a row; in each aligned block of 48 rows (0 to 47, 48 to 95, ...) at most 4 rows name the same one
- gate_probs: float32 [1536, 8], P('ep'), may hold values from 0.02 to 0.3
- gate_codes: bfloat16 [4096, 131072], P(None, ('ep', 'rep')), may hold values from -0.09375 to 0.09375
- gate_scales: float32 [32, 1024], P(None, ('ep', 'rep')), may hold values from 0.5 to 2
- up_codes: bfloat16 [4096, 131072], P(None, ('ep', 'rep')), may hold values from -0.09375 to 0.09375
- up_scales: float32 [32, 1024], P(None, ('ep', 'rep')), may hold values from 0.5 to 2
- down_codes: bfloat16 [131072, 4096], P(('ep', 'rep')), may hold values from -0.1875 to 0.1875
- down_scales: float32 [1024, 32], P(('ep', 'rep')), may hold values from 0.5 to 2
Outputs:
- mixed: bfloat16 [1536, 4096], P('ep', 'rep')
- d_tokens: bfloat16 [1536, 4096], P('ep', 'rep')
The draws below stay inside these ranges and needn't reach their ends.
Inputs may be any that keep to these rules, and one draw needn't show every extreme that they name: `routes`: each row names 8 different experts. Among the 48 rows of one device (the aligned blocks of 48 rows), no expert is named more than 4 times, and in every draw some expert is named exactly 4 times within one block.
All inputs are finite; a program needn't handle non-finite values.
Results may differ from the reference program's by a relative error of at most 0.022.
Values may be sent and summed in bfloat16 or wider, within the bound.
A program may use at most 64 MiB of HBM per device.

```python
import math
import jax
import jax.numpy as jnp
import numpy as np
from jax import lax

D = 4096
FF = 1024
TOP = 8
BLK = 128
TOK_EP = 48
SHARDS = 8
FF_DEV = 128
EXPERTS = 128
CAP = 4
TOKENS = 1536
N_EP = 32


def block_scale(rng, shape, shards, least, top_value):
    def one(position, shards_of):
        heights = jax.random.uniform(jax.random.fold_in(jax.random.fold_in(rng, 6), position), (shards_of,), jnp.float32, least / len(shards), top_value / len(shards))
        return jnp.repeat(jnp.exp(heights), shape[position] // shards_of).reshape((-1,) + (1,) * (len(shape) - position - 1))

    loudness = one(*shards[0])
    for cut in shards[1:]:
        loudness = loudness * one(*cut)
    return loudness


def assign_block(key, own, number, rows, amount, top, bound, skew):
    order = jax.random.permutation(key, amount)
    heavy_load, usual = portions_of(amount, rows * top, bound, skew, True), portions_of(amount, rows * top, bound, skew, False)
    places = jnp.arange(amount)

    def named(sizes, offset_by):
        used = int((sizes > 0).sum())
        fixed = max(1, used // 4)
        moved = fixed + (places - fixed + offset_by * (used - fixed)) % max(1, amount - fixed)
        return jnp.zeros((amount,), jnp.int32).at[order[jnp.where(places < fixed, places, moved)]].set(jnp.asarray(sizes, jnp.int32))

    sizes = jnp.where(number % 4 == 0, named(heavy_load, number // 4), named(usual, number - number // 4 - 1))
    mixed = jax.random.permutation(jax.random.fold_in(own, 3), amount)
    source_of, taker = mixed[0:amount // 2 * 2:2], mixed[1:amount // 2 * 2:2]
    slack = jnp.minimum(sizes[source_of] - 1, bound - sizes[taker]) // 2
    slack = jnp.where((source_of == order[0]) | (taker == order[0]) | (sizes[taker] == 0), 0, jnp.maximum(slack, 0))
    moved = jax.random.randint(jax.random.fold_in(own, 4), (amount // 2,), 0, 1 << 20) % (slack + 1)
    sizes = sizes.at[source_of].add(-moved).at[taker].add(moved)
    labels = jnp.searchsorted(jnp.cumsum(sizes), jnp.arange(rows * top), side="right").astype(jnp.int32)
    listing = labels.reshape(top, rows).T
    listing = listing[jax.random.permutation(jax.random.fold_in(own, 1), rows)]
    offset_by = jax.random.randint(jax.random.fold_in(own, 2), (rows, 1), 0, top)
    return jnp.take_along_axis(listing, (jnp.arange(top)[None, :] + offset_by) % top, axis=1)


def portions_of(number_of, total, most, skew, full):
    weights = [(1 << 20) // math.isqrt(rank ** skew) + 1 for rank in range(1, number_of + 1)]
    largest = most if full else min(most, max(-(-total // number_of), total * weights[0] // sum(weights)))
    least = 1 if total - largest >= number_of - 1 else 0
    holding, surplus = [largest] + [least] * (number_of - 1), total - largest - least * (number_of - 1)
    while surplus > 0:
        candidates = [i for i in range(1, number_of) if holding[i] < largest] or [i for i in range(1, number_of) if holding[i] < most]
        mass, left = sum([weights[i] for i in candidates]), surplus
        for i in candidates:
            more = min(most - holding[i], max(1, left * weights[i] // mass), surplus)
            holding[i] = holding[i] + more
            surplus = surplus - more
    return np.array(holding)


def centred(key, shape, spread, bound, split=(), held_as=jnp.bfloat16):
    drawn = spread * jax.random.normal(key, shape, jnp.float32)
    if split:
        drawn = drawn * block_scale(key, shape, split, -0.22, 0.18)
    return jnp.clip(drawn, -bound, bound).astype(held_as)


def setup_inputs(seed: int = 0) -> dict:
    splits = jax.random.split(jax.random.key(seed), 11)
    tokens = centred(splits[0], (TOKENS, D), 1.0, 6.0, ((0, 32),))
    cotangent = centred(splits[1], (TOKENS, D), 1.0, 6.0, ((0, 32),))
    routes_keys = jax.random.split(jax.random.fold_in(splits[2], 1), TOKENS // TOK_EP)
    routes_turns = jax.random.permutation(jax.random.fold_in(splits[2], 3), TOKENS // TOK_EP)
    routes = jax.vmap(lambda own, number: assign_block(jax.random.fold_in(splits[2], 2), own, number, TOK_EP, EXPERTS, TOP, CAP, 2))(routes_keys, routes_turns).reshape((TOKENS, TOP))
    gate_probs = jnp.clip(jnp.exp(math.log(0.3) - 2.7080503 * jax.random.uniform(splits[3], (TOKENS, TOP), jnp.float32) ** block_scale(splits[3], (TOKENS, TOP), ((0, 32),), -0.2, 0.2)), 0.02, 0.3)
    gate_codes = centred(splits[4], (D, EXPERTS * FF), D ** -0.5, 0.09375, ((1, 1024),))
    gate_scales = jnp.clip(jnp.exp(math.log(2.0) - 1.3862944 * jax.random.uniform(splits[5], (D // BLK, EXPERTS * FF // BLK), jnp.float32) ** block_scale(splits[5], (D // BLK, EXPERTS * FF // BLK), ((1, 1024),), -0.2, 0.2)), 0.5, 2.0)
    up_codes = centred(splits[6], (D, EXPERTS * FF), D ** -0.5, 0.09375, ((1, 1024),))
    up_scales = jnp.clip(jnp.exp(math.log(2.0) - 1.3862944 * jax.random.uniform(splits[7], (D // BLK, EXPERTS * FF // BLK), jnp.float32) ** block_scale(splits[7], (D // BLK, EXPERTS * FF // BLK), ((1, 1024),), -0.2, 0.2)), 0.5, 2.0)
    down_codes = centred(splits[8], (EXPERTS * FF, D), FF ** -0.5, 0.1875, ((0, 1024),))
    down_scales = jnp.clip(jnp.exp(math.log(2.0) - 1.3862944 * jax.random.uniform(splits[9], (EXPERTS * FF // BLK, D // BLK), jnp.float32) ** block_scale(splits[9], (EXPERTS * FF // BLK, D // BLK), ((0, 1024),), -0.2, 0.2)), 0.5, 2.0)
    return dict(tokens=tokens, cotangent=cotangent, routes=routes, gate_probs=gate_probs, gate_codes=gate_codes, gate_scales=gate_scales, up_codes=up_codes, up_scales=up_scales, down_codes=down_codes, down_scales=down_scales)


def expanded(scales):
    return jnp.repeat(jnp.repeat(scales, BLK, axis=0), BLK, axis=1)


def silu_parts(gate_act):
    sigmoid = jax.nn.sigmoid(gate_act)
    return gate_act * sigmoid, sigmoid * (1.0 + gate_act * (1.0 - sigmoid))


def reference(tokens, cotangent, routes, gate_probs, gate_codes, gate_scales, up_codes, up_scales, down_codes, down_scales):
    highest = lax.Precision.HIGHEST
    flattened = routes.reshape(N_EP, TOK_EP * TOP)
    onehot = (flattened[:, :, None] == jnp.arange(EXPERTS, dtype=jnp.int32)[None, None, :]).astype(jnp.int32)
    before = jnp.cumsum(onehot, axis=1) - onehot
    slot_rank = jnp.sum(before * onehot, axis=2).reshape(N_EP, TOK_EP, TOP)
    grouped = flattened.reshape(N_EP, TOK_EP, TOP)
    weights_of = gate_probs.astype(jnp.float32).reshape(N_EP, TOK_EP, TOP)
    token_values = tokens.astype(jnp.float32).reshape(N_EP, TOK_EP, D)
    cot_values = cotangent.astype(jnp.float32).reshape(N_EP, TOK_EP, D)
    slot_iota = jnp.arange(CAP, dtype=jnp.int32)
    rows_all = N_EP * CAP

    def one_expert(carry, expert):
        out_sum, dx_sum = carry
        matches = (grouped == expert)[:, None, :, :] & (slot_rank[:, None, :, :] == slot_iota[None, :, None, None])
        chosen = jnp.any(matches, axis=3).astype(jnp.float32)
        weighted = jnp.sum(jnp.where(matches, weights_of[:, None, :, :], 0.0), axis=3)
        slot_rows = jnp.einsum("sct,std->scd", chosen, token_values, precision=highest).astype(jnp.bfloat16).reshape(rows_all, D)
        slot_grads = jnp.einsum("sct,std->scd", weighted, cot_values, precision=highest).astype(jnp.bfloat16).reshape(rows_all, D)
        column_start = (expert * FF).astype(jnp.int32)
        scale_start = (expert * (FF // BLK)).astype(jnp.int32)
        w_gate = (lax.dynamic_slice_in_dim(gate_codes, column_start, FF, 1).astype(jnp.float32) * expanded(lax.dynamic_slice_in_dim(gate_scales, scale_start, FF // BLK, 1))).astype(jnp.bfloat16)
        w_up = (lax.dynamic_slice_in_dim(up_codes, column_start, FF, 1).astype(jnp.float32) * expanded(lax.dynamic_slice_in_dim(up_scales, scale_start, FF // BLK, 1))).astype(jnp.bfloat16)
        w_down = (lax.dynamic_slice_in_dim(down_codes, column_start, FF, 0).astype(jnp.float32) * expanded(lax.dynamic_slice_in_dim(down_scales, scale_start, FF // BLK, 0))).astype(jnp.bfloat16)
        gate_act = jnp.dot(slot_rows, w_gate, preferred_element_type=jnp.float32)
        up_act = jnp.dot(slot_rows, w_up, preferred_element_type=jnp.float32)
        activation, derivative = silu_parts(gate_act)
        hidden = (activation * up_act).astype(jnp.bfloat16)
        hidden_parts = hidden.astype(jnp.float32).reshape(rows_all, SHARDS, FF_DEV)
        down_parts = w_down.astype(jnp.float32).reshape(SHARDS, FF_DEV, D)
        out_terms = jnp.einsum("rsf,sfd->srd", hidden_parts, down_parts, precision=highest).astype(jnp.bfloat16)
        hidden_grad = lax.dot_general(slot_grads, w_down, (((1,), (1,)), ((), ())), preferred_element_type=jnp.float32)
        gate_grad = (hidden_grad * up_act * derivative).astype(jnp.bfloat16)
        up_grad = (hidden_grad * activation).astype(jnp.bfloat16)
        gate_parts = w_gate.astype(jnp.float32).reshape(D, SHARDS, FF_DEV)
        up_parts = w_up.astype(jnp.float32).reshape(D, SHARDS, FF_DEV)
        dx_terms = (jnp.einsum("rsf,dsf->srd", gate_grad.astype(jnp.float32).reshape(rows_all, SHARDS, FF_DEV), gate_parts, precision=highest)
                    + jnp.einsum("rsf,dsf->srd", up_grad.astype(jnp.float32).reshape(rows_all, SHARDS, FF_DEV), up_parts, precision=highest)).astype(jnp.bfloat16)
        out_rows = jnp.sum(out_terms.astype(jnp.float32), axis=0).reshape(N_EP, CAP, D)
        dx_rows = jnp.sum(dx_terms.astype(jnp.float32), axis=0).reshape(N_EP, CAP, D)
        out_sum = out_sum + jnp.einsum("sct,scd->std", chosen, out_rows, precision=highest)
        dx_sum = dx_sum + jnp.einsum("sct,scd->std", chosen, dx_rows, precision=highest)
        return (out_sum, dx_sum), None

    zeros = jnp.zeros((N_EP, TOK_EP, D), jnp.float32)
    (out_sum, dx_sum), _ = lax.scan(one_expert, (zeros, zeros), jnp.arange(EXPERTS, dtype=jnp.int32))
    mixed = out_sum.reshape(TOKENS, D).astype(jnp.bfloat16)
    d_tokens = dx_sum.reshape(TOKENS, D).astype(jnp.bfloat16)
    return mixed, d_tokens
```

```python
import jax
import jax.numpy as jnp
from jax import lax
from jax.experimental import pallas as pl
from jax.experimental.pallas import tpu as pltpu
from jax.sharding import PartitionSpec as P

EXP_EP = 4
TOP = 8
BLK = 128
CAP = 4
ROWS = 16
MESH = pl.DeviceIdType.MESH
NT = (((1,), (1,)), ((), ()))
F32 = jnp.float32
BF16 = jnp.bfloat16


def dot(a, b):
    return jnp.dot(a, b, preferred_element_type=F32)


def kernel(
    n,
    tok,
    cot,
    routes,
    probs,
    gate_s,
    up_s,
    down_s,
    gate_c,
    up_c,
    down_c,
    mixed,
    d_tok,
    raw_g,
    raw_u,
    raw_d,
    w_gu,
    w_d,
    sel,
    send,
    x_all,
    acc_gu,
    acc_d,
    hid,
    grad,
    term,
    from_sib,
    from_nbr,
    pair,
    back,
    fin,
    fin_in,
    load_sem,
    eps,
    epr,
    share_s,
    share_r,
    red_s,
    red_r,
    eps2,
    epr2,
    fin_s,
    fin_r,
):
    s = lax.axis_index("ep")
    r = lax.axis_index("rep")
    core = lax.rem(r, 2)
    xp = lax.rem(r // 2, 2)
    g = lax.rem(r, 4)
    u = r // 4
    block = r // 8
    sib = (s, r + 1 - 2 * core)
    nbr = (s, r + 2 - 4 * xp)
    tok_rows, width = tok.shape
    half = width // 2
    quarter = width // 4
    lanes = 2 * BLK

    def peer(k):
        return lax.rem(s + k, n)

    loads = [
        pltpu.make_async_copy(src, dst, load_sem.at[i])
        for i, (src, dst) in enumerate(((gate_c, raw_g), (up_c, raw_u), (down_c, raw_d)))
    ]
    for load in loads:
        load.start()

    barrier = pltpu.get_barrier_semaphore()

    def greet(k, carry):
        pl.semaphore_signal(barrier, inc=1, device_id=(peer(k), r), device_id_type=MESH)
        return carry

    def greet_final(v, carry):
        pl.semaphore_signal(
            barrier, inc=1, device_id=(s, lax.rem(u + v, 8) * 4 + g), device_id_type=MESH
        )
        return carry

    lax.fori_loop(1, n, greet, 0)
    lax.fori_loop(1, 8, greet_final, 0)
    pl.semaphore_signal(barrier, inc=1, device_id=sib, device_id_type=MESH)
    pl.semaphore_signal(barrier, inc=1, device_id=nbr, device_id_type=MESH)

    rows8 = n * 8
    ri = lax.broadcasted_iota(jnp.int32, (rows8, tok_rows), 0)
    away = s + ri // 8
    away = jnp.where(away >= n, away - n, away)
    wanted = (EXP_EP * away + block).astype(F32)
    eye = (
        lax.broadcasted_iota(jnp.int32, (TOP, TOP), 0)
        == lax.broadcasted_iota(jnp.int32, (TOP, TOP), 1)
    ).astype(F32)
    routes_f = routes[...].astype(F32)
    routes_t = lax.dot_general(
        eye, routes_f, NT, precision=lax.Precision.HIGHEST, preferred_element_type=F32
    )
    probs_t = lax.dot_general(
        eye, probs[...], NT, precision=lax.Precision.HIGHEST, preferred_element_type=F32
    )
    named = jnp.zeros((rows8, tok_rows), F32)
    weight = jnp.zeros((rows8, tok_rows), F32)
    for k in range(TOP):
        hit = jnp.abs(routes_t[k : k + 1, :] - wanted) < 0.5
        named = jnp.where(hit, 1.0, named)
        weight = jnp.where(hit, probs_t[k : k + 1, :], weight)
    ti = lax.broadcasted_iota(jnp.int32, (tok_rows, tok_rows), 0)
    tj = lax.broadcasted_iota(jnp.int32, (tok_rows, tok_rows), 1)
    rank = dot(named.astype(BF16), (ti < tj).astype(F32).astype(BF16))
    slot = lax.rem(ri, CAP).astype(F32)
    chosen = jnp.where(rank == slot, named, 0.0)
    array_of = lax.rem(ri // CAP, 2)
    row_weight = jnp.sum(chosen * jnp.where(array_of == 0, 1.0, weight), axis=1, keepdims=True)
    pick_tok = jnp.where(array_of == 0, chosen, 0.0).astype(BF16)
    pick_cot = jnp.where(array_of == 1, chosen, 0.0).astype(BF16)

    def piece(ref, start):
        lo = pl.multiple_of(start, BLK)
        hi = pl.multiple_of(start + quarter, BLK)
        return jnp.concatenate([ref[:, pl.ds(lo, BLK)], ref[:, pl.ds(hi, BLK)]], axis=1)

    for h in range(2):
        parts = []
        for q in range(2):
            start = q * half + (4 * h + g) * BLK
            rows = dot(pick_tok, piece(tok, start)) + dot(pick_cot, piece(cot, start))
            parts.append((rows * row_weight).reshape(n, 8, lanes))
        send[h] = jnp.concatenate(parts, axis=1).astype(BF16)
        x_all[4 * h + g, 0] = send[h, 0]

    pl.semaphore_wait(barrier, n - 1 + 7 + 2)

    for h in range(2):

        def go(k, carry, h=h):
            pltpu.make_async_remote_copy(
                src_ref=send.at[h, k],
                dst_ref=x_all.at[4 * h + g, k],
                send_sem=eps.at[h],
                recv_sem=epr.at[h],
                device_id=(peer(k), r),
                device_id_type=MESH,
            ).start()
            return carry

        lax.fori_loop(1, n, go, 0)

    rows16 = n * ROWS
    li = lax.broadcasted_iota(jnp.int32, (tok_rows, rows16), 1)
    away = s + li // ROWS
    away = jnp.where(away >= n, away - n, away)
    wanted = EXP_EP * away + block
    named = jnp.zeros((tok_rows, rows16), F32)
    for k in range(TOP):
        named = jnp.where(routes[:, k : k + 1] == wanted, 1.0, named)
    rank = dot((tj < ti).astype(F32).astype(BF16), named.astype(BF16))
    chosen = jnp.where(rank == lax.rem(li, CAP).astype(F32), named, 0.0)
    kind = lax.rem(li // CAP, 4)
    for i in range(4):
        sel[i * tok_rows : (i + 1) * tok_rows, :] = jnp.where(kind == i, chosen, 0.0).astype(BF16)

    for load in loads:
        load.wait()

    def expand(ch, carry):
        j = lax.rem(ch, 8)
        at = pl.ds(pl.multiple_of((ch // 8) * BLK, BLK), BLK)
        src = pl.ds(pl.multiple_of(ch * BLK, BLK), BLK)
        w_gu[j, at, 0:BLK] = (raw_g[src, :].astype(F32) * gate_s[ch, 0]).astype(BF16)
        w_gu[j, at, BLK : 2 * BLK] = (raw_u[src, :].astype(F32) * up_s[ch, 0]).astype(BF16)
        w_d[j, :, at] = (raw_d[:, src].astype(F32) * down_s[0, ch]).astype(BF16)
        return carry

    lax.fori_loop(0, width // BLK, expand, 0)

    acc_gu[...] = jnp.zeros_like(acc_gu)
    acc_d[...] = jnp.zeros_like(acc_d)

    def first(j):
        got = x_all[j].astype(F32)
        flat = jnp.concatenate(
            [got[:, 0:8].reshape(rows8, lanes), got[:, 8:16].reshape(rows8, lanes)], axis=1
        ).astype(BF16)
        acc_gu[...] += dot(flat, w_gu[j])
        acc_d[...] += lax.dot_general(flat, w_d[j], NT, preferred_element_type=F32)

    def bulk_wait(ref, sem):
        pltpu.make_async_copy(ref, ref, sem).wait()

    def share(h, way):
        j = 4 * h + (g if way < 2 else g + 2 - 4 * xp)
        return pltpu.make_async_remote_copy(
            src_ref=x_all.at[j],
            dst_ref=x_all.at[j],
            send_sem=share_s.at[h, way],
            recv_sem=share_r.at[h, way],
            device_id=nbr if way == 1 else sib,
            device_id_type=MESH,
        )

    def arrived(h, way):
        j = 4 * h + (
            (g + 1 - 2 * core, g + 2 - 4 * xp, g + 1 - 2 * core + 2 - 4 * xp)[way]
        )
        bulk_wait(x_all.at[j], share_r.at[h, way])
        return j

    def own(h):
        bulk_wait(x_all.at[4 * h + g, pl.ds(1, n - 1)], epr.at[h])
        for way in (1, 0):
            share(h, way).start()
        return 4 * h + g

    j = own(0)
    first(j)
    j = arrived(0, 0)
    first(j)
    j1 = own(1)
    j = arrived(0, 1)
    share(0, 2).start()
    first(j1)
    first(j)
    j = arrived(1, 0)
    first(j)
    j = arrived(0, 2)
    first(j)
    j = arrived(1, 1)
    share(1, 2).start()
    first(j)
    j = arrived(1, 2)
    first(j)

    gate = acc_gu[:, 0:BLK].reshape(n, 8, BLK)
    up = acc_gu[:, BLK : 2 * BLK].reshape(n, 8, BLK)
    hid_grad = acc_d[...].reshape(n, 8, BLK)
    grad_row = lax.broadcasted_iota(jnp.int32, (n, 8, BLK), 1) >= CAP
    sigmoid = jax.nn.sigmoid(gate)
    act = gate * sigmoid
    slope = sigmoid * (1.0 + gate * (1.0 - sigmoid))

    def swap(v):
        return jnp.concatenate([v[:, CAP:], v[:, :CAP]], axis=1)

    hid[...] = jnp.where(grad_row, 0.0, act * up).reshape(rows8, BLK).astype(BF16)
    gate_grad = jnp.where(grad_row, hid_grad * swap(up * slope), 0.0)
    up_grad = jnp.where(grad_row, hid_grad * swap(act), 0.0)
    grad[:, 0:BLK] = gate_grad.reshape(rows8, BLK).astype(BF16)
    grad[:, BLK : 2 * BLK] = up_grad.reshape(rows8, BLK).astype(BF16)

    def second(j):
        rows = dot(hid[...], w_d[j]) + lax.dot_general(
            grad[...], w_gu[j], NT, preferred_element_type=F32
        )
        return jnp.concatenate(
            [rows[:, :lanes].reshape(n, 8, lanes), rows[:, lanes:].reshape(n, 8, lanes)], axis=1
        )

    def to_sib(h, kept):
        xq = xp if kept else 1 - xp
        i = 2 * h + kept
        term[i] = second(4 * h + 2 * xq + 1 - core).astype(BF16)
        copy = pltpu.make_async_remote_copy(
            src_ref=term.at[i],
            dst_ref=from_sib.at[i],
            send_sem=red_s.at[i],
            recv_sem=red_r.at[i],
            device_id=sib,
            device_id_type=MESH,
        )
        copy.start()
        return copy

    sib_copies = {}
    nbr_copies = {}
    for h in range(2):
        sib_copies[h, 0] = to_sib(h, 0)
    for h in range(2):
        value = second(4 * h + 2 * (1 - xp) + core)
        sib_copies[h, 0].wait_recv()
        pair[2 + h] = (value + from_sib[2 * h].astype(F32)).astype(BF16)
        nbr_copies[h] = pltpu.make_async_remote_copy(
            src_ref=pair.at[2 + h],
            dst_ref=from_nbr.at[h],
            send_sem=red_s.at[4 + h],
            recv_sem=red_r.at[4 + h],
            device_id=nbr,
            device_id_type=MESH,
        )
        nbr_copies[h].start()
    for h in range(2):
        sib_copies[h, 1] = to_sib(h, 1)
    for h in range(2):
        value = second(4 * h + 2 * xp + core)
        sib_copies[h, 1].wait_recv()
        value = value + from_sib[2 * h + 1].astype(F32)
        nbr_copies[h].wait_recv()
        pair[h] = (value + from_nbr[h].astype(F32)).astype(BF16)

        def go_back(k, carry, h=h):
            pltpu.make_async_remote_copy(
                src_ref=pair.at[h, k],
                dst_ref=back.at[h, k],
                send_sem=eps2.at[h],
                recv_sem=epr2.at[h],
                device_id=(lax.rem(s + n - k, n), r),
                device_id_type=MESH,
            ).start()
            return carry

        lax.fori_loop(1, n, go_back, 0)
        back[h, 0] = pair[h, 0]

    for h in range(2):
        bulk_wait(back.at[h, pl.ds(1, n - 1)], epr2.at[h])
        sums = dot(sel[...], back[h].reshape(rows16, lanes))
        for q in range(2):
            for b in range(2):
                fin[4 * q + 2 * b + h] = sums[
                    q * 2 * tok_rows : (q + 1) * 2 * tok_rows, b * BLK : (b + 1) * BLK
                ].astype(BF16)

    def go_final(v, carry):
        to = lax.rem(u + v, 8)
        pltpu.make_async_remote_copy(
            src_ref=fin.at[to],
            dst_ref=fin_in.at[v],
            send_sem=fin_s.at[v],
            recv_sem=fin_r,
            device_id=(s, to * 4 + g),
            device_id_type=MESH,
        ).start()
        return carry

    lax.fori_loop(1, 8, go_final, 0)
    bulk_wait(fin_in.at[pl.ds(1, 7)], fin_r)
    total = fin[u].astype(F32)
    for v in range(1, 8):
        total = total + fin_in[v].astype(F32)
    mixed[...] = total[:tok_rows].astype(BF16)
    d_tok[...] = total[tok_rows:].astype(BF16)

    def sent(v, carry):
        bulk_wait(fin.at[v], fin_s.at[v])
        return carry

    lax.fori_loop(1, 8, sent, 0)
    for h in range(2):
        bulk_wait(send.at[h, pl.ds(1, n - 1)], eps.at[h])
        bulk_wait(pair.at[h, pl.ds(1, n - 1)], eps2.at[h])
        for way in range(3):
            share(h, way).wait_send()
        nbr_copies[h].wait_send()
        for kept in range(2):
            sib_copies[h, kept].wait_send()


def per_device(
    tokens,
    cotangent,
    routes,
    gate_probs,
    gate_codes,
    gate_scales,
    up_codes,
    up_scales,
    down_codes,
    down_scales,
):
    n = lax.axis_size("ep")
    tok_rows, width = tokens.shape
    lanes = 2 * BLK
    vmem = pl.BlockSpec(memory_space=pltpu.VMEM)
    smem = pl.BlockSpec(memory_space=pltpu.SMEM)
    hbm = pl.BlockSpec(memory_space=pl.ANY)
    out = jax.ShapeDtypeStruct((tok_rows, BLK), BF16)
    dma = pltpu.SemaphoreType.DMA

    def body(*refs):
        kernel(n, *refs)

    return pl.pallas_call(
        body,
        out_shape=(out, out),
        in_specs=[vmem] * 4 + [smem] * 3 + [hbm] * 3,
        out_specs=(vmem, vmem),
        scratch_shapes=[
            pltpu.VMEM((width, BLK), BF16),
            pltpu.VMEM((width, BLK), BF16),
            pltpu.VMEM((BLK, width), BF16),
            pltpu.VMEM((8, 4 * BLK, 2 * BLK), BF16),
            pltpu.VMEM((8, BLK, 4 * BLK), BF16),
            pltpu.VMEM((4 * tok_rows, n * ROWS), BF16),
            pltpu.VMEM((2, n, ROWS, lanes), BF16),
            pltpu.VMEM((8, n, ROWS, lanes), BF16),
            pltpu.VMEM((n * 8, 2 * BLK), F32),
            pltpu.VMEM((n * 8, BLK), F32),
            pltpu.VMEM((n * 8, BLK), BF16),
            pltpu.VMEM((n * 8, 2 * BLK), BF16),
            pltpu.VMEM((4, n, ROWS, lanes), BF16),
            pltpu.VMEM((4, n, ROWS, lanes), BF16),
            pltpu.VMEM((2, n, ROWS, lanes), BF16),
            pltpu.VMEM((4, n, ROWS, lanes), BF16),
            pltpu.VMEM((2, n, ROWS, lanes), BF16),
            pltpu.VMEM((8, 2 * tok_rows, BLK), BF16),
            pltpu.VMEM((8, 2 * tok_rows, BLK), BF16),
            dma((3,)),
            dma((2,)),
            dma((2,)),
            dma((2, 3)),
            dma((2, 3)),
            dma((6,)),
            dma((6,)),
            dma((2,)),
            dma((2,)),
            dma((8,)),
            dma,
        ],
        compiler_params=pltpu.CompilerParams(
            collective_id=0, has_side_effects=True, vmem_limit_bytes=40 * 1024 * 1024
        ),
        cost_estimate=pl.CostEstimate(
            flops=2 * 9 * n * 8 * width * BLK,
            bytes_accessed=2 * 3 * width * BLK,
            transcendentals=n * 8 * BLK,
        ),
    )(
        tokens,
        cotangent,
        routes,
        gate_probs,
        gate_scales,
        up_scales,
        down_scales,
        gate_codes,
        up_codes,
        down_codes,
    )


def solution(mesh):
    placed = (
        P("ep", None),
        P("ep", None),
        P("ep", None),
        P("ep", None),
        P(None, ("ep", "rep")),
        P(None, ("ep", "rep")),
        P(None, ("ep", "rep")),
        P(None, ("ep", "rep")),
        P(("ep", "rep"), None),
        P(("ep", "rep"), None),
    )
    return jax.shard_map(
        per_device,
        mesh=mesh,
        in_specs=placed,
        out_specs=(P("ep", "rep"), P("ep", "rep")),
        check_vma=False,
    )
```

```python
import jax
import jax.numpy as jnp
from jax import lax
from jax.experimental import pallas as pl
from jax.experimental.pallas import tpu as pltpu
from jax.sharding import PartitionSpec as P

EXP_EP = 4
TOP = 8
BLK = 128
CAP = 4
ROWS = 16
MESH = pl.DeviceIdType.MESH
NT = (((1,), (1,)), ((), ()))
F32 = jnp.float32
BF16 = jnp.bfloat16


def dot(a, b):
    return jnp.dot(a, b, preferred_element_type=F32)


def kernel(
    n,
    tok_h,
    cot_h,
    routes_h,
    probs_h,
    gate_sh,
    up_sh,
    down_sh,
    gate_c,
    up_c,
    down_c,
    mixed,
    d_tok,
    tok,
    cot,
    routes,
    probs,
    gate_s,
    up_s,
    down_s,
    raw_g,
    raw_u,
    raw_d,
    w_gu,
    w_d,
    sel,
    send,
    x_all,
    acc_gu,
    acc_d,
    hid,
    grad,
    term,
    from_sib,
    from_nbr,
    pair,
    mine,
    back,
    fin,
    fin_in,
    load_sem,
    eps,
    epr,
    share_s,
    share_r,
    red_s,
    red_r,
    eps2,
    epr2,
    fin_s,
    fin_r,
):
    s = lax.axis_index("ep")
    r = lax.axis_index("rep")
    core = lax.rem(r, 2)
    xp = lax.rem(r // 2, 2)
    g = lax.rem(r, 4)
    u = r // 4
    block = r // 8
    sib = (s, r + 1 - 2 * core)
    nbr = (s, r + 2 - 4 * xp)
    tok_rows, width = tok.shape
    half = width // 2
    quarter = width // 4
    lanes = 2 * BLK

    def away_of(i):
        k = jnp.where(lax.rem(i, 2) == 1, (i + 1) // 2, n - i // 2)
        return lax.rem(s + k, n)

    def back_of(i):
        k = jnp.where(lax.rem(i, 2) == 1, (i + 1) // 2, n - i // 2)
        return lax.rem(s + n - k, n)

    def part(p):
        return pl.ds(p * (n // 2), n // 2)

    pairs = (
        (routes_h, routes),
        (probs_h, probs),
        (tok_h, tok),
        (cot_h, cot),
        (gate_sh, gate_s),
        (up_sh, up_s),
        (down_sh, down_s),
        (gate_c, raw_g),
        (up_c, raw_u),
        (down_c, raw_d),
    )
    loads = [
        pltpu.make_async_copy(src, dst, load_sem.at[i]) for i, (src, dst) in enumerate(pairs)
    ]
    for load in loads:
        load.start()

    barrier = pltpu.get_barrier_semaphore()

    def greet(k, carry):
        pl.semaphore_signal(barrier, inc=1, device_id=(away_of(k), r), device_id_type=MESH)
        return carry

    def greet_final(v, carry):
        pl.semaphore_signal(
            barrier, inc=1, device_id=(s, lax.rem(u + v, 8) * 4 + g), device_id_type=MESH
        )
        return carry

    lax.fori_loop(1, n, greet, 0)
    lax.fori_loop(1, 8, greet_final, 0)
    pl.semaphore_signal(barrier, inc=1, device_id=sib, device_id_type=MESH)
    pl.semaphore_signal(barrier, inc=1, device_id=nbr, device_id_type=MESH)

    for load in loads[:4]:
        load.wait()

    rows8 = n * 8
    ri = lax.broadcasted_iota(jnp.int32, (rows8, tok_rows), 0)
    away = away_of(ri // 8)
    wanted = (EXP_EP * away + block).astype(F32)
    eye = (
        lax.broadcasted_iota(jnp.int32, (TOP, TOP), 0)
        == lax.broadcasted_iota(jnp.int32, (TOP, TOP), 1)
    ).astype(F32)
    routes_f = routes[...].astype(F32)
    routes_t = lax.dot_general(
        routes_f,
        eye,
        (((0,), (0,)), ((), ())),
        precision=lax.Precision.HIGHEST,
        preferred_element_type=F32,
    )
    named = jnp.zeros((rows8, tok_rows), F32)
    weight = jnp.zeros((rows8, tok_rows), F32)
    for k in range(TOP):
        hit = jnp.abs(routes_f[k : k + 1, :] - wanted) < 0.5
        named = jnp.where(hit, 1.0, named)
        weight = jnp.where(hit, probs[k : k + 1, :], weight)
    ti = lax.broadcasted_iota(jnp.int32, (tok_rows, tok_rows), 0)
    tj = lax.broadcasted_iota(jnp.int32, (tok_rows, tok_rows), 1)
    rank = dot(named.astype(BF16), (ti < tj).astype(F32).astype(BF16))
    slot = lax.rem(ri, CAP).astype(F32)
    chosen = jnp.where(rank == slot, named, 0.0)
    array_of = lax.rem(ri // CAP, 2)
    row_weight = jnp.sum(chosen * jnp.where(array_of == 0, 1.0, weight), axis=1, keepdims=True)
    pick_tok = jnp.where(array_of == 0, chosen, 0.0).astype(BF16)
    pick_cot = jnp.where(array_of == 1, chosen, 0.0).astype(BF16)

    def piece(ref, start):
        lo = pl.multiple_of(start, BLK)
        hi = pl.multiple_of(start + quarter, BLK)
        return jnp.concatenate([ref[:, pl.ds(lo, BLK)], ref[:, pl.ds(hi, BLK)]], axis=1)

    for h in range(2):
        parts = []
        for q in range(2):
            start = q * half + (4 * h + g) * BLK
            rows = dot(pick_tok, piece(tok, start)) + dot(pick_cot, piece(cot, start))
            parts.append((rows * row_weight).reshape(n, 8, lanes))
        send[h] = jnp.concatenate(parts, axis=1).astype(BF16)
        x_all[4 * h + g, 0] = send[h, 0]
        if h == 0:
            pl.semaphore_wait(barrier, n - 1 + 7 + 2)
        for p in range(2):

            def go(i, carry, h=h, p=p):
                pltpu.make_async_remote_copy(
                    src_ref=send.at[h, i],
                    dst_ref=x_all.at[4 * h + g, i],
                    send_sem=eps.at[h],
                    recv_sem=epr.at[h, p],
                    device_id=(away_of(i), r),
                    device_id_type=MESH,
                ).start()
                return carry

            lax.fori_loop(max(1, p * (n // 2)), (p + 1) * (n // 2), go, 0)

    rows16 = n * ROWS
    li = lax.broadcasted_iota(jnp.int32, (tok_rows, rows16), 1)
    away = away_of(li // ROWS)
    wanted = (EXP_EP * away + block).astype(F32)
    named = jnp.zeros((tok_rows, rows16), F32)
    for k in range(TOP):
        named = jnp.where(jnp.abs(routes_t[:, k : k + 1] - wanted) < 0.5, 1.0, named)
    rank = dot((tj < ti).astype(F32).astype(BF16), named.astype(BF16))
    chosen = jnp.where(rank == lax.rem(li, CAP).astype(F32), named, 0.0)
    kind = lax.rem(li // CAP, 4)
    for i in range(4):
        sel[i * tok_rows : (i + 1) * tok_rows, :] = jnp.where(kind == i, chosen, 0.0).astype(BF16)

    for load in loads[4:]:
        load.wait()

    def expand(ch, carry):
        j = lax.rem(ch, 8)
        at = pl.ds(pl.multiple_of((ch // 8) * BLK, BLK), BLK)
        src = pl.ds(pl.multiple_of(ch * BLK, BLK), BLK)
        w_gu[j, at, 0:BLK] = (raw_g[src, :].astype(F32) * gate_s[0, ch]).astype(BF16)
        w_gu[j, at, BLK : 2 * BLK] = (raw_u[src, :].astype(F32) * up_s[0, ch]).astype(BF16)
        w_d[j, :, at] = (raw_d[:, src].astype(F32) * down_s[0, ch]).astype(BF16)
        return carry

    lax.fori_loop(0, width // BLK, expand, 0)

    acc_gu[...] = jnp.zeros_like(acc_gu)
    acc_d[...] = jnp.zeros_like(acc_d)

    def first(j):
        got = x_all[j].astype(F32)
        flat = jnp.concatenate(
            [got[:, 0:8].reshape(rows8, lanes), got[:, 8:16].reshape(rows8, lanes)], axis=1
        ).astype(BF16)
        acc_gu[...] += dot(flat, w_gu[j])
        acc_d[...] += lax.dot_general(flat, w_d[j], NT, preferred_element_type=F32)

    def bulk_wait(ref, sem):
        pltpu.make_async_copy(ref, ref, sem).wait()

    def landed(p):
        return pl.ds(1, n // 2 - 1) if p == 0 else part(1)

    def share(h, p, way):
        j = 4 * h + (g if way < 2 else g + 2 - 4 * xp)
        return pltpu.make_async_remote_copy(
            src_ref=x_all.at[j, part(p)],
            dst_ref=x_all.at[j, part(p)],
            send_sem=share_s.at[h, p, way],
            recv_sem=share_r.at[h, p, way],
            device_id=nbr if way == 1 else sib,
            device_id_type=MESH,
        )

    def source(h, way):
        return 4 * h + (
            (g + 1 - 2 * core, g + 2 - 4 * xp, g + 1 - 2 * core + 2 - 4 * xp)[way]
        )

    def arrived(h, p, way):
        bulk_wait(x_all.at[source(h, way), part(p)], share_r.at[h, p, way])

    def own(h, p):
        bulk_wait(x_all.at[4 * h + g, landed(p)], epr.at[h, p])
        share(h, p, 1).start()
        share(h, p, 0).start()

    def forward(h, p):
        arrived(h, p, 1)
        share(h, p, 2).start()

    def take(h, way):
        for p in range(2):
            arrived(h, p, way)
        first(source(h, way))

    own(0, 0)
    own(0, 1)
    first(g)
    forward(0, 0)
    take(0, 0)
    own(1, 0)
    forward(0, 1)
    first(source(0, 1))
    own(1, 1)
    first(4 + g)
    forward(1, 0)
    take(0, 2)
    take(1, 0)
    forward(1, 1)
    first(source(1, 1))
    take(1, 2)

    gate = acc_gu[:, 0:BLK].reshape(n, 8, BLK)
    up = acc_gu[:, BLK : 2 * BLK].reshape(n, 8, BLK)
    hid_grad = acc_d[...].reshape(n, 8, BLK)
    grad_row = lax.broadcasted_iota(jnp.int32, (n, 8, BLK), 1) >= CAP
    sigmoid = jax.nn.sigmoid(gate)
    act = gate * sigmoid
    slope = sigmoid * (1.0 + gate * (1.0 - sigmoid))

    def swap(v):
        return jnp.concatenate([v[:, CAP:], v[:, :CAP]], axis=1)

    hid[...] = jnp.where(grad_row, 0.0, act * up).reshape(rows8, BLK).astype(BF16)
    gate_grad = jnp.where(grad_row, hid_grad * swap(up * slope), 0.0)
    up_grad = jnp.where(grad_row, hid_grad * swap(act), 0.0)
    grad[:, 0:BLK] = gate_grad.reshape(rows8, BLK).astype(BF16)
    grad[:, BLK : 2 * BLK] = up_grad.reshape(rows8, BLK).astype(BF16)

    def second(j):
        rows = dot(hid[...], w_d[j]) + lax.dot_general(
            grad[...], w_gu[j], NT, preferred_element_type=F32
        )
        return jnp.concatenate(
            [rows[:, :lanes].reshape(n, 8, lanes), rows[:, lanes:].reshape(n, 8, lanes)], axis=1
        )

    def to_sib(h, kept):
        xq = xp if kept else 1 - xp
        i = 2 * h + kept
        term[i] = second(4 * h + 2 * xq + 1 - core).astype(BF16)
        copy = pltpu.make_async_remote_copy(
            src_ref=term.at[i],
            dst_ref=from_sib.at[i],
            send_sem=red_s.at[i],
            recv_sem=red_r.at[i],
            device_id=sib,
            device_id_type=MESH,
        )
        copy.start()
        return copy

    sib_copies = {}
    nbr_copies = {}
    for h in range(2):
        sib_copies[h, 0] = to_sib(h, 0)
    for h in range(2):
        value = second(4 * h + 2 * (1 - xp) + core)
        sib_copies[h, 0].wait_recv()
        pair[2 + h] = (value + from_sib[2 * h].astype(F32)).astype(BF16)
        for p in range(2):
            nbr_copies[h, p] = pltpu.make_async_remote_copy(
                src_ref=pair.at[2 + h, part(p)],
                dst_ref=from_nbr.at[h, part(p)],
                send_sem=red_s.at[4 + 2 * h + p],
                recv_sem=red_r.at[4 + 2 * h + p],
                device_id=nbr,
                device_id_type=MESH,
            )
            nbr_copies[h, p].start()
    for h in range(2):
        sib_copies[h, 1] = to_sib(h, 1)
    for h in range(2):
        value = second(4 * h + 2 * xp + core)
        sib_copies[h, 1].wait_recv()
        mine[h] = value + from_sib[2 * h + 1].astype(F32)
    for h in range(2):
        for p in range(2):
            nbr_copies[h, p].wait_recv()
            pair[h, part(p)] = (
                mine[h, part(p)] + from_nbr[h, part(p)].astype(F32)
            ).astype(BF16)

            def go_back(i, carry, h=h, p=p):
                pltpu.make_async_remote_copy(
                    src_ref=pair.at[h, i],
                    dst_ref=back.at[h, i],
                    send_sem=eps2.at[h],
                    recv_sem=epr2.at[h, p],
                    device_id=(back_of(i), r),
                    device_id_type=MESH,
                ).start()
                return carry

            lax.fori_loop(max(1, p * (n // 2)), (p + 1) * (n // 2), go_back, 0)
        back[h, 0] = pair[h, 0]

    half_rows = rows16 // 2
    for h in range(2):
        sums = None
        for p in range(2):
            bulk_wait(back.at[h, landed(p)], epr2.at[h, p])
            more = dot(
                sel[:, p * half_rows : (p + 1) * half_rows],
                back[h, part(p)].reshape(half_rows, lanes),
            )
            sums = more if p == 0 else sums + more
        for q in range(2):
            for b in range(2):
                fin[4 * q + 2 * b + h] = sums[
                    q * 2 * tok_rows : (q + 1) * 2 * tok_rows, b * BLK : (b + 1) * BLK
                ].astype(BF16)

        def go_final(w, carry, h=h):
            to = 2 * w + h

            @pl.when(to != u)
            def _():
                pltpu.make_async_remote_copy(
                    src_ref=fin.at[to],
                    dst_ref=fin_in.at[lax.rem(to + 8 - u, 8)],
                    send_sem=fin_s,
                    recv_sem=fin_r,
                    device_id=(s, to * 4 + g),
                    device_id_type=MESH,
                ).start()

            return carry

        lax.fori_loop(0, 4, go_final, 0)
    bulk_wait(fin_in.at[pl.ds(1, 7)], fin_r)
    total = fin[u].astype(F32)
    for v in range(1, 8):
        total = total + fin_in[v].astype(F32)
    mixed[...] = total[:tok_rows].astype(BF16)
    d_tok[...] = total[tok_rows:].astype(BF16)

    bulk_wait(fin_in.at[pl.ds(1, 7)], fin_s)
    for h in range(2):
        bulk_wait(send.at[h, pl.ds(1, n - 1)], eps.at[h])
        bulk_wait(pair.at[h, pl.ds(1, n - 1)], eps2.at[h])
        for p in range(2):
            for way in range(3):
                share(h, p, way).wait_send()
            nbr_copies[h, p].wait_send()
        for kept in range(2):
            sib_copies[h, kept].wait_send()


def per_device(
    tokens,
    cotangent,
    routes,
    gate_probs,
    gate_codes,
    gate_scales,
    up_codes,
    up_scales,
    down_codes,
    down_scales,
):
    n = lax.axis_size("ep")
    tok_rows, width = tokens.shape
    lanes = 2 * BLK
    vmem = pl.BlockSpec(memory_space=pltpu.VMEM)
    hbm = pl.BlockSpec(memory_space=pl.ANY)
    out = jax.ShapeDtypeStruct((tok_rows, BLK), BF16)
    dma = pltpu.SemaphoreType.DMA

    def body(*refs):
        kernel(n, *refs)

    return pl.pallas_call(
        body,
        out_shape=(out, out),
        in_specs=[hbm] * 10,
        out_specs=(vmem, vmem),
        scratch_shapes=[
            pltpu.VMEM((tok_rows, width), BF16),
            pltpu.VMEM((tok_rows, width), BF16),
            pltpu.VMEM((TOP, tok_rows), jnp.int32),
            pltpu.VMEM((TOP, tok_rows), F32),
            pltpu.SMEM((1, width // BLK), F32),
            pltpu.SMEM((1, width // BLK), F32),
            pltpu.SMEM((1, width // BLK), F32),
            pltpu.VMEM((width, BLK), BF16),
            pltpu.VMEM((width, BLK), BF16),
            pltpu.VMEM((BLK, width), BF16),
            pltpu.VMEM((8, 4 * BLK, 2 * BLK), BF16),
            pltpu.VMEM((8, BLK, 4 * BLK), BF16),
            pltpu.VMEM((4 * tok_rows, n * ROWS), BF16),
            pltpu.VMEM((2, n, ROWS, lanes), BF16),
            pltpu.VMEM((8, n, ROWS, lanes), BF16),
            pltpu.VMEM((n * 8, 2 * BLK), F32),
            pltpu.VMEM((n * 8, BLK), F32),
            pltpu.VMEM((n * 8, BLK), BF16),
            pltpu.VMEM((n * 8, 2 * BLK), BF16),
            pltpu.VMEM((4, n, ROWS, lanes), BF16),
            pltpu.VMEM((4, n, ROWS, lanes), BF16),
            pltpu.VMEM((2, n, ROWS, lanes), BF16),
            pltpu.VMEM((4, n, ROWS, lanes), BF16),
            pltpu.VMEM((2, n, ROWS, lanes), F32),
            pltpu.VMEM((2, n, ROWS, lanes), BF16),
            pltpu.VMEM((8, 2 * tok_rows, BLK), BF16),
            pltpu.VMEM((8, 2 * tok_rows, BLK), BF16),
            dma((10,)),
            dma((2,)),
            dma((2, 2)),
            dma((2, 2, 3)),
            dma((2, 2, 3)),
            dma((8,)),
            dma((8,)),
            dma((2,)),
            dma((2, 2)),
            dma,
            dma,
        ],
        compiler_params=pltpu.CompilerParams(
            collective_id=0, has_side_effects=True, vmem_limit_bytes=60 * 1024 * 1024
        ),
        cost_estimate=pl.CostEstimate(
            flops=2 * 9 * n * 8 * width * BLK,
            bytes_accessed=2 * 3 * width * BLK,
            transcendentals=n * 8 * BLK,
        ),
    )(
        tokens,
        cotangent,
        routes.T,
        gate_probs.T,
        gate_scales.T,
        up_scales.T,
        down_scales,
        gate_codes,
        up_codes,
        down_codes,
    )


def solution(mesh):
    placed = (
        P("ep", None),
        P("ep", None),
        P("ep", None),
        P("ep", None),
        P(None, ("ep", "rep")),
        P(None, ("ep", "rep")),
        P(None, ("ep", "rep")),
        P(None, ("ep", "rep")),
        P(("ep", "rep"), None),
        P(("ep", "rep"), None),
    )
    return jax.shard_map(
        per_device,
        mesh=mesh,
        in_specs=placed,
        out_specs=(P("ep", "rep"), P("ep", "rep")),
        check_vma=False,
    )
```

```python
import jax
import jax.numpy as jnp
from jax import lax
from jax.experimental import pallas as pl
from jax.experimental.pallas import tpu as pltpu
from jax.sharding import PartitionSpec as P

EXP_EP = 4
TOP = 8
BLK = 128
CAP = 4
PARTS = 4
ROWS = 16
MESH = pl.DeviceIdType.MESH
NT = (((1,), (1,)), ((), ()))
F32 = jnp.float32
BF16 = jnp.bfloat16


def dot(a, b):
    return jnp.dot(a, b, preferred_element_type=F32)


def kernel(
    n,
    tok_h,
    cot_h,
    routes_h,
    probs_h,
    gate_sh,
    up_sh,
    down_sh,
    gate_c,
    up_c,
    down_c,
    sums_out,
    tok,
    cot,
    routes,
    probs,
    gate_s,
    up_s,
    down_s,
    raw_g,
    raw_u,
    raw_d,
    w_gu,
    w_d,
    sel,
    send,
    x_all,
    acc_gu,
    acc_d,
    hid,
    grad,
    term,
    from_sib,
    from_nbr,
    pair,
    mine,
    back,
    fin,
    fin_in,
    load_sem,
    eps,
    epr,
    share_s,
    share_r,
    red_s,
    red_r,
    eps2,
    epr2,
    fin_s,
    fin_r,
):
    s = lax.axis_index("ep")
    r = lax.axis_index("rep")
    core = lax.rem(r, 2)
    xp = lax.rem(r // 2, 2)
    g = lax.rem(r, 4)
    u = r // 4
    block = r // 8
    sib = (s, r + 1 - 2 * core)
    nbr = (s, r + 2 - 4 * xp)
    tok_rows, width = tok.shape
    half = width // 2
    quarter = width // 4
    lanes = 2 * BLK

    def away_of(i):
        k = jnp.where(lax.rem(i, 2) == 1, (i + 1) // 2, n - i // 2)
        return lax.rem(s + k, n)

    def back_of(i):
        k = jnp.where(lax.rem(i, 2) == 1, (i + 1) // 2, n - i // 2)
        return lax.rem(s + n - k, n)

    def part(p):
        return pl.ds(p * (n // PARTS), n // PARTS)

    pairs = (
        (routes_h, routes),
        (probs_h, probs),
        (tok_h, tok),
        (cot_h, cot),
        (gate_sh, gate_s),
        (up_sh, up_s),
        (down_sh, down_s),
        (gate_c, raw_g),
        (up_c, raw_u),
        (down_c, raw_d),
    )
    loads = [
        pltpu.make_async_copy(src, dst, load_sem.at[i]) for i, (src, dst) in enumerate(pairs)
    ]
    for load in loads:
        load.start()

    barrier = pltpu.get_barrier_semaphore()

    def greet(k, carry):
        pl.semaphore_signal(barrier, inc=1, device_id=(away_of(k), r), device_id_type=MESH)
        return carry

    def greet_final(v, carry):
        pl.semaphore_signal(
            barrier, inc=1, device_id=(s, lax.rem(u + v, 8) * 4 + g), device_id_type=MESH
        )
        return carry

    lax.fori_loop(1, n, greet, 0)
    lax.fori_loop(1, 8, greet_final, 0)
    pl.semaphore_signal(barrier, inc=1, device_id=sib, device_id_type=MESH)
    pl.semaphore_signal(barrier, inc=1, device_id=nbr, device_id_type=MESH)

    for load in loads[:2]:
        load.wait()

    rows8 = n * 8
    ri = lax.broadcasted_iota(jnp.int32, (rows8, tok_rows), 0)
    away = away_of(ri // 8)
    wanted = (EXP_EP * away + block).astype(F32)
    eye = (
        lax.broadcasted_iota(jnp.int32, (TOP, TOP), 0)
        == lax.broadcasted_iota(jnp.int32, (TOP, TOP), 1)
    ).astype(F32)
    routes_f = routes[...].astype(F32)
    routes_t = lax.dot_general(
        routes_f,
        eye,
        (((0,), (0,)), ((), ())),
        precision=lax.Precision.HIGHEST,
        preferred_element_type=F32,
    )
    named = jnp.zeros((rows8, tok_rows), F32)
    weight = jnp.zeros((rows8, tok_rows), F32)
    for k in range(TOP):
        hit = jnp.abs(routes_f[k : k + 1, :] - wanted) < 0.5
        named = jnp.where(hit, 1.0, named)
        weight = jnp.where(hit, probs[k : k + 1, :], weight)
    ti = lax.broadcasted_iota(jnp.int32, (tok_rows, tok_rows), 0)
    tj = lax.broadcasted_iota(jnp.int32, (tok_rows, tok_rows), 1)
    rank = dot(named.astype(BF16), (ti < tj).astype(F32).astype(BF16))
    slot = lax.rem(ri, CAP).astype(F32)
    chosen = jnp.where(rank == slot, named, 0.0)
    array_of = lax.rem(ri // CAP, 2)
    row_weight = jnp.sum(chosen * jnp.where(array_of == 0, 1.0, weight), axis=1, keepdims=True)
    pick_tok = jnp.where(array_of == 0, chosen, 0.0).astype(BF16)
    pick_cot = jnp.where(array_of == 1, chosen, 0.0).astype(BF16)

    def piece(ref, start):
        lo = pl.multiple_of(start, BLK)
        hi = pl.multiple_of(start + quarter, BLK)
        return jnp.concatenate([ref[:, pl.ds(lo, BLK)], ref[:, pl.ds(hi, BLK)]], axis=1)

    for load in loads[2:4]:
        load.wait()

    for h in range(2):
        parts = []
        for q in range(2):
            start = q * half + (4 * h + g) * BLK
            rows = dot(pick_tok, piece(tok, start)) + dot(pick_cot, piece(cot, start))
            parts.append((rows * row_weight).reshape(n, 8, lanes))
        send[h] = jnp.concatenate(parts, axis=1).astype(BF16)
        x_all[4 * h + g, 0] = send[h, 0]
        if h == 0:
            pl.semaphore_wait(barrier, n - 1 + 7 + 2)
        for p in range(PARTS):

            def go(i, carry, h=h, p=p):
                pltpu.make_async_remote_copy(
                    src_ref=send.at[h, i],
                    dst_ref=x_all.at[4 * h + g, i],
                    send_sem=eps.at[h],
                    recv_sem=epr.at[h, p],
                    device_id=(away_of(i), r),
                    device_id_type=MESH,
                ).start()
                return carry

            lax.fori_loop(max(1, p * (n // PARTS)), (p + 1) * (n // PARTS), go, 0)

    rows16 = n * ROWS
    li = lax.broadcasted_iota(jnp.int32, (tok_rows, rows16), 1)
    away = away_of(li // ROWS)
    wanted = (EXP_EP * away + block).astype(F32)
    named = jnp.zeros((tok_rows, rows16), F32)
    for k in range(TOP):
        named = jnp.where(jnp.abs(routes_t[:, k : k + 1] - wanted) < 0.5, 1.0, named)
    rank = dot((tj < ti).astype(F32).astype(BF16), named.astype(BF16))
    chosen = jnp.where(rank == lax.rem(li, CAP).astype(F32), named, 0.0)
    kind = lax.rem(li // CAP, 4)
    for i in range(4):
        sel[i * tok_rows : (i + 1) * tok_rows, :] = jnp.where(kind == i, chosen, 0.0).astype(BF16)

    for load in loads[4:]:
        load.wait()

    def expand(ch, carry):
        j = lax.rem(ch, 8)
        at = pl.ds(pl.multiple_of((ch // 8) * BLK, BLK), BLK)
        src = pl.ds(pl.multiple_of(ch * BLK, BLK), BLK)
        w_gu[j, at, 0:BLK] = (raw_g[src, :].astype(F32) * gate_s[0, ch]).astype(BF16)
        w_gu[j, at, BLK : 2 * BLK] = (raw_u[src, :].astype(F32) * up_s[0, ch]).astype(BF16)
        w_d[j, :, at] = (raw_d[:, src].astype(F32) * down_s[0, ch]).astype(BF16)
        return carry

    lax.fori_loop(0, width // BLK, expand, 0)

    acc_gu[...] = jnp.zeros_like(acc_gu)
    acc_d[...] = jnp.zeros_like(acc_d)

    def first(j):
        got = x_all[j].astype(F32)
        flat = jnp.concatenate(
            [got[:, 0:8].reshape(rows8, lanes), got[:, 8:16].reshape(rows8, lanes)], axis=1
        ).astype(BF16)
        acc_gu[...] += dot(flat, w_gu[j])
        acc_d[...] += lax.dot_general(flat, w_d[j], NT, preferred_element_type=F32)

    def bulk_wait(ref, sem):
        pltpu.make_async_copy(ref, ref, sem).wait()

    def landed(p):
        return pl.ds(1, n // PARTS - 1) if p == 0 else part(p)

    def share(h, p, way):
        j = 4 * h + (g if way < 2 else g + 2 - 4 * xp)
        return pltpu.make_async_remote_copy(
            src_ref=x_all.at[j, part(p)],
            dst_ref=x_all.at[j, part(p)],
            send_sem=share_s.at[h, p, way],
            recv_sem=share_r.at[h, p, way],
            device_id=nbr if way == 1 else sib,
            device_id_type=MESH,
        )

    def source(h, way):
        return 4 * h + (
            (g + 1 - 2 * core, g + 2 - 4 * xp, g + 1 - 2 * core + 2 - 4 * xp)[way]
        )

    def arrived(h, p, way):
        bulk_wait(x_all.at[source(h, way), part(p)], share_r.at[h, p, way])

    def own(h, p):
        bulk_wait(x_all.at[4 * h + g, landed(p)], epr.at[h, p])
        share(h, p, 1).start()
        share(h, p, 0).start()

    def forward(h, p):
        arrived(h, p, 1)
        share(h, p, 2).start()

    def take(h, way):
        for p in range(PARTS):
            arrived(h, p, way)
        first(source(h, way))

    for t in range(2 * PARTS):
        own(t // PARTS, t % PARTS)
        if t > 0:
            forward((t - 1) // PARTS, (t - 1) % PARTS)
        if t == PARTS + 1:
            first(g)
            take(0, 0)
        if t == PARTS + 2:
            first(source(0, 1))
            take(0, 2)
    first(4 + g)
    take(1, 0)
    forward(1, PARTS - 1)
    first(source(1, 1))
    take(1, 2)

    gate = acc_gu[:, 0:BLK].reshape(n, 8, BLK)
    up = acc_gu[:, BLK : 2 * BLK].reshape(n, 8, BLK)
    hid_grad = acc_d[...].reshape(n, 8, BLK)
    grad_row = lax.broadcasted_iota(jnp.int32, (n, 8, BLK), 1) >= CAP
    sigmoid = jax.nn.sigmoid(gate)
    act = gate * sigmoid
    slope = sigmoid * (1.0 + gate * (1.0 - sigmoid))

    def swap(v):
        return jnp.concatenate([v[:, CAP:], v[:, :CAP]], axis=1)

    hid[...] = jnp.where(grad_row, 0.0, act * up).reshape(rows8, BLK).astype(BF16)
    gate_grad = jnp.where(grad_row, hid_grad * swap(up * slope), 0.0)
    up_grad = jnp.where(grad_row, hid_grad * swap(act), 0.0)
    grad[:, 0:BLK] = gate_grad.reshape(rows8, BLK).astype(BF16)
    grad[:, BLK : 2 * BLK] = up_grad.reshape(rows8, BLK).astype(BF16)

    def second(j):
        rows = dot(hid[...], w_d[j]) + lax.dot_general(
            grad[...], w_gu[j], NT, preferred_element_type=F32
        )
        return jnp.concatenate(
            [rows[:, :lanes].reshape(n, 8, lanes), rows[:, lanes:].reshape(n, 8, lanes)], axis=1
        )

    def to_sib(h, kept):
        xq = xp if kept else 1 - xp
        i = 2 * h + kept
        term[i] = second(4 * h + 2 * xq + 1 - core).astype(BF16)
        copy = pltpu.make_async_remote_copy(
            src_ref=term.at[i],
            dst_ref=from_sib.at[i],
            send_sem=red_s.at[i],
            recv_sem=red_r.at[i],
            device_id=sib,
            device_id_type=MESH,
        )
        copy.start()
        return copy

    sib_copies = {}
    nbr_copies = {}
    for h in range(2):
        sib_copies[h, 0] = to_sib(h, 0)
    for h in range(2):
        value = second(4 * h + 2 * (1 - xp) + core)
        sib_copies[h, 0].wait_recv()
        pair[2 + h] = (value + from_sib[2 * h].astype(F32)).astype(BF16)
        for p in range(PARTS):
            nbr_copies[h, p] = pltpu.make_async_remote_copy(
                src_ref=pair.at[2 + h, part(p)],
                dst_ref=from_nbr.at[h, part(p)],
                send_sem=red_s.at[4 + PARTS * h + p],
                recv_sem=red_r.at[4 + PARTS * h + p],
                device_id=nbr,
                device_id_type=MESH,
            )
            nbr_copies[h, p].start()
    for h in range(2):
        sib_copies[h, 1] = to_sib(h, 1)
    for h in range(2):
        value = second(4 * h + 2 * xp + core)
        sib_copies[h, 1].wait_recv()
        mine[h] = value + from_sib[2 * h + 1].astype(F32)
    for h in range(2):
        for p in range(PARTS):
            nbr_copies[h, p].wait_recv()
            pair[h, part(p)] = (
                mine[h, part(p)] + from_nbr[h, part(p)].astype(F32)
            ).astype(BF16)

            def go_back(i, carry, h=h, p=p):
                pltpu.make_async_remote_copy(
                    src_ref=pair.at[h, i],
                    dst_ref=back.at[h, i],
                    send_sem=eps2.at[h],
                    recv_sem=epr2.at[h, p],
                    device_id=(back_of(i), r),
                    device_id_type=MESH,
                ).start()
                return carry

            lax.fori_loop(max(1, p * (n // PARTS)), (p + 1) * (n // PARTS), go_back, 0)
        back[h, 0] = pair[h, 0]

    part_rows = rows16 // PARTS
    for h in range(2):
        sums = None
        for p in range(PARTS):
            bulk_wait(back.at[h, landed(p)], epr2.at[h, p])
            more = dot(
                sel[:, p * part_rows : (p + 1) * part_rows],
                back[h, part(p)].reshape(part_rows, lanes),
            )
            sums = more if p == 0 else sums + more
        for q in range(2):
            for b in range(2):
                fin[4 * q + 2 * b + h] = sums[
                    q * 2 * tok_rows : (q + 1) * 2 * tok_rows, b * BLK : (b + 1) * BLK
                ].astype(BF16)

        def go_final(w, carry, h=h):
            to = 2 * w + h

            @pl.when(to != u)
            def _():
                pltpu.make_async_remote_copy(
                    src_ref=fin.at[to],
                    dst_ref=fin_in.at[lax.rem(to + 8 - u, 8)],
                    send_sem=fin_s,
                    recv_sem=fin_r,
                    device_id=(s, to * 4 + g),
                    device_id_type=MESH,
                ).start()

            return carry

        lax.fori_loop(0, 4, go_final, 0)
    bulk_wait(fin_in.at[pl.ds(1, 7)], fin_r)
    total = fin[u].astype(F32)
    for v in range(1, 8):
        total = total + fin_in[v].astype(F32)
    sums_out[...] = total.astype(BF16)

    bulk_wait(fin_in.at[pl.ds(1, 7)], fin_s)
    for h in range(2):
        bulk_wait(send.at[h, pl.ds(1, n - 1)], eps.at[h])
        bulk_wait(pair.at[h, pl.ds(1, n - 1)], eps2.at[h])
        for p in range(PARTS):
            for way in range(3):
                share(h, p, way).wait_send()
            nbr_copies[h, p].wait_send()
        for kept in range(2):
            sib_copies[h, kept].wait_send()


def per_device(
    tokens,
    cotangent,
    routes,
    gate_probs,
    gate_codes,
    gate_scales,
    up_codes,
    up_scales,
    down_codes,
    down_scales,
):
    n = lax.axis_size("ep")
    tok_rows, width = tokens.shape
    lanes = 2 * BLK
    vmem = pl.BlockSpec(memory_space=pltpu.VMEM)
    hbm = pl.BlockSpec(memory_space=pl.ANY)
    out = jax.ShapeDtypeStruct((2 * tok_rows, BLK), BF16)
    dma = pltpu.SemaphoreType.DMA

    def body(*refs):
        kernel(n, *refs)

    sums = pl.pallas_call(
        body,
        out_shape=out,
        in_specs=[hbm] * 10,
        out_specs=vmem,
        scratch_shapes=[
            pltpu.VMEM((tok_rows, width), BF16),
            pltpu.VMEM((tok_rows, width), BF16),
            pltpu.VMEM((TOP, tok_rows), jnp.int32),
            pltpu.VMEM((TOP, tok_rows), F32),
            pltpu.SMEM((1, width // BLK), F32),
            pltpu.SMEM((1, width // BLK), F32),
            pltpu.SMEM((1, width // BLK), F32),
            pltpu.VMEM((width, BLK), BF16),
            pltpu.VMEM((width, BLK), BF16),
            pltpu.VMEM((BLK, width), BF16),
            pltpu.VMEM((8, 4 * BLK, 2 * BLK), BF16),
            pltpu.VMEM((8, BLK, 4 * BLK), BF16),
            pltpu.VMEM((4 * tok_rows, n * ROWS), BF16),
            pltpu.VMEM((2, n, ROWS, lanes), BF16),
            pltpu.VMEM((8, n, ROWS, lanes), BF16),
            pltpu.VMEM((n * 8, 2 * BLK), F32),
            pltpu.VMEM((n * 8, BLK), F32),
            pltpu.VMEM((n * 8, BLK), BF16),
            pltpu.VMEM((n * 8, 2 * BLK), BF16),
            pltpu.VMEM((4, n, ROWS, lanes), BF16),
            pltpu.VMEM((4, n, ROWS, lanes), BF16),
            pltpu.VMEM((2, n, ROWS, lanes), BF16),
            pltpu.VMEM((4, n, ROWS, lanes), BF16),
            pltpu.VMEM((2, n, ROWS, lanes), F32),
            pltpu.VMEM((2, n, ROWS, lanes), BF16),
            pltpu.VMEM((8, 2 * tok_rows, BLK), BF16),
            pltpu.VMEM((8, 2 * tok_rows, BLK), BF16),
            dma((10,)),
            dma((2,)),
            dma((2, PARTS)),
            dma((2, PARTS, 3)),
            dma((2, PARTS, 3)),
            dma((4 + 2 * PARTS,)),
            dma((4 + 2 * PARTS,)),
            dma((2,)),
            dma((2, PARTS)),
            dma,
            dma,
        ],
        compiler_params=pltpu.CompilerParams(
            collective_id=0, has_side_effects=True, vmem_limit_bytes=60 * 1024 * 1024
        ),
        cost_estimate=pl.CostEstimate(
            flops=2 * 9 * n * 8 * width * BLK,
            bytes_accessed=2 * 3 * width * BLK,
            transcendentals=n * 8 * BLK,
        ),
    )(
        tokens,
        cotangent,
        routes.T,
        gate_probs.T,
        gate_scales.T,
        up_scales.T,
        down_scales,
        gate_codes,
        up_codes,
        down_codes,
    )
    return sums[:tok_rows], sums[tok_rows:]


def solution(mesh):
    placed = (
        P("ep", None),
        P("ep", None),
        P("ep", None),
        P("ep", None),
        P(None, ("ep", "rep")),
        P(None, ("ep", "rep")),
        P(None, ("ep", "rep")),
        P(None, ("ep", "rep")),
        P(("ep", "rep"), None),
        P(("ep", "rep"), None),
    )
    return jax.shard_map(
        per_device,
        mesh=mesh,
        in_specs=placed,
        out_specs=(P("ep", "rep"), P("ep", "rep")),
        check_vma=False,
    )
```
